32 devices in a mesh: row: 4 (over y, x), col: 4 (over z), depth: 2 (over core).
Axes of the slice: x: 2, y: 2, z: 4, core: 2. Of those that a mesh axis runs over, the one named last changes fastest.
Arguments:
- tokens: bfloat16 [512, 12288], P(('col', 'depth'), 'row'), may hold values from -6 to 6
- weight: bfloat16 [12288, 24576], P('row', ('col', 'depth')), may hold values from -0.0546875 to 0.0546875
- cotangent: bfloat16 [512, 24576], P('row', ('col', 'depth')), may hold values from -6 to 6
Outputs:
- hidden: bfloat16 [512, 24576], P('row', ('col', 'depth'))
- input_grad: bfloat16 [512, 12288], P(('col', 'depth'), 'row')
- weight_grad: float32 [12288, 24576], P('row', ('col', 'depth'))
The draws below stay inside these ranges and needn't reach their ends.
All inputs are finite; a program needn't handle non-finite values.
Results may differ from the reference program's by a relative error of at most 0.02.
Values may be sent and summed in bfloat16 or wider, within the bound.
A program may use at most 192 MiB of HBM per device.

```python
import jax
import jax.numpy as jnp
from jax import lax

D = 12288
FF = 24576
TOKENS = 512
FB = 3072
N_COL = 4
N_DEPTH = 2


def level_of(stream_key, shape, split, low, largest):
    gain, own = 1.0, jax.random.fold_in(stream_key, 6)
    for position, shards_of in split:
        steps = jnp.exp(jax.random.uniform(jax.random.fold_in(own, position), (shards_of,), jnp.float32, low / len(split), largest / len(split)))
        gain = gain * jnp.repeat(steps, shape[position] // shards_of).reshape([-1 if axis == position else 1 for axis in range(len(shape))])
    return gain


def gaussian(key, extent, spread, limit, shards=(), dtype=jnp.bfloat16):
    factor_of = level_of(key, extent, shards, -0.22, 0.18) if shards else 1.0
    entries = jax.random.normal(key, extent, jnp.float32) * spread * factor_of
    return jnp.minimum(jnp.maximum(entries, -limit), limit).astype(dtype)


def setup_inputs(seed: int = 0) -> dict:
    keys = jax.random.split(jax.random.key(seed), 4)
    return {
        "tokens": gaussian(keys[0], (TOKENS, D), 1.0, 6.0, ((0, 8), (1, 4))),
        "weight": gaussian(keys[1], (D, FF), D ** -0.5, 0.0546875, ((0, 4), (1, 8))),
        "cotangent": gaussian(keys[2], (TOKENS, FF), 1.0, 6.0, ((0, 4), (1, 8))),
    }


root_coef = 0.7978845608
cubic_coef = 0.044715


def gelu_parts(preact):
    inner = root_coef * (preact + cubic_coef * preact * preact * preact)
    tanh_val = jnp.tanh(inner)
    value = 0.5 * preact * (1.0 + tanh_val)
    slope = 0.5 * (1.0 + tanh_val) + 0.5 * preact * (1.0 - tanh_val * tanh_val) * root_coef * (1.0 + 3.0 * cubic_coef * preact * preact)
    return value, slope


def reference(tokens, weight, cotangent):
    preact = jnp.dot(tokens, weight, preferred_element_type=jnp.float32)
    value, slope = gelu_parts(preact)
    hidden = value.astype(jnp.bfloat16)
    grad_pre = (cotangent.astype(jnp.float32) * slope).astype(jnp.bfloat16)
    token_count = tokens.shape[0]
    weight_grad = lax.dot_general(tokens, grad_pre, (((0,), (0,)), ((), ())), preferred_element_type=jnp.float32) * (token_count ** -0.5)
    block_count = N_COL * N_DEPTH
    grad_blocks = grad_pre.reshape(token_count, block_count, FB).transpose(1, 0, 2)
    weight_blocks = weight.reshape(D, block_count, FB).transpose(1, 0, 2)

    def add_block(carry, pieces):
        grad_piece, weight_piece = pieces
        product = lax.dot_general(grad_piece, weight_piece, (((1,), (1,)), ((), ())), preferred_element_type=jnp.float32)
        rounded = lax.optimization_barrier(product.astype(jnp.bfloat16))
        return carry + rounded.astype(jnp.float32), None

    start_sum = jnp.zeros((token_count, D), jnp.float32)
    grad_sum, _ = lax.scan(add_block, start_sum, (grad_blocks, weight_blocks))
    return hidden, grad_sum.astype(jnp.bfloat16), weight_grad
```

```python
import functools

import jax
import jax.numpy as jnp
from jax import lax
from jax.experimental import pallas as pl
from jax.experimental.pallas import tpu as pltpu
from jax.sharding import PartitionSpec as P

MESH = pl.DeviceIdType.MESH
root_coef = 0.7978845608
cubic_coef = 0.044715
chunks = 2


def gelu_parts(preact):
    inner = root_coef * (preact + cubic_coef * preact * preact * preact)
    tanh_val = jnp.tanh(inner)
    value = 0.5 * preact * (1.0 + tanh_val)
    slope = 0.5 * (1.0 + tanh_val) + 0.5 * preact * (1.0 - tanh_val * tanh_val) * root_coef * (
        1.0 + 3.0 * cubic_coef * preact * preact
    )
    return (value, slope)


def tile_of(extent, most):
    return max(t for t in range(128, min(most, extent) + 1, 128) if extent % t == 0)


def chain_kernel(
    n_row, n_col, n_depth, f_tile, d_tile,
    tok_ref, w_hbm, cot_ref,
    hid_ref, ing_ref, x_ref, g_ref,
    w_ref, part_ref, relay_a, relay_b, sum_a, sum_b, from_x, from_y,
    back_ref, sib_ref, chip_ref, line_ref,
    w_sem, own_sem,
    line_send, sib_send, x_recv,
    rs_send, rs_recv, ag_send, ag_recv,
    sb_send, sb_recv, zl_send, zl_recv,
):
    f32, bf16 = jnp.float32, jnp.bfloat16
    row, col, depth = lax.axis_index("row"), lax.axis_index("col"), lax.axis_index("depth")
    blocks = n_col * n_depth
    own_tokens, d_size = tok_ref.shape
    f_size = cot_ref.shape[1]
    piece = own_tokens // chunks
    chunk_rows = blocks * piece
    row_rows = chunk_rows // n_row
    half = row_rows // 2
    per_row = blocks // n_row
    nf, nd = f_size // f_tile, d_size // d_tile

    row_x = row + 1 - 2 * lax.rem(row, 2)
    row_y = lax.rem(row + 2, 4)
    row_z = lax.rem(row_x + 2, 4)
    dev_x = (row_x, col, depth)
    dev_y = (row_y, col, depth)
    cols = [lax.rem(col + o, n_col) for o in range(n_col)]
    depths = [lax.rem(depth + o, n_depth) for o in range(n_depth)]
    dev_c = [(row, c, depth) for c in cols]
    dev_d = [(row, col, d) for d in depths]

    sends = []

    def push(src, dst, send_sem, recv_sem, device):
        copy = pltpu.make_async_remote_copy(
            src_ref=src, dst_ref=dst, send_sem=send_sem, recv_sem=recv_sem,
            device_id=device, device_id_type=MESH,
        )
        copy.start()
        sends.append(copy)

    def arrived(dst, recv_sem):
        pltpu.make_async_remote_copy(
            src_ref=dst, dst_ref=dst, send_sem=recv_sem, recv_sem=recv_sem,
            device_id=dev_x, device_id_type=MESH,
        ).wait_recv()

    def al(v, m):
        return pl.multiple_of(v, m)

    def x_at(k, block):
        return x_ref.at[pl.ds(al(k * chunk_rows + block * piece, piece), piece), :]

    def rows_at(ref, k, r, j, part=None):
        start = k * chunk_rows + r * row_rows
        size = row_rows
        if part is not None:
            start, size = start + part * half, half
        return ref.at[pl.ds(al(start, half), size), pl.ds(j * f_tile, f_tile)]

    def half_at(ref, k, j):
        return ref.at[pl.ds(k * half, half), pl.ds(j * f_tile, f_tile)]

    def sum_at(ref, k, j, part):
        return ref.at[pl.ds(k * row_rows + part * half, half), pl.ds(j * f_tile, f_tile)]

    weight_copy = pltpu.make_async_copy(w_hbm, w_ref, w_sem)
    weight_copy.start()

    barrier = pltpu.get_barrier_semaphore()
    greet = dev_c[1:] + dev_d[1:] + [dev_x, dev_y]
    for device in greet:
        pl.semaphore_signal(barrier, inc=1, device_id=device, device_id_type=MESH)
    pl.semaphore_wait(barrier, len(greet))

    me = col * n_depth + depth
    own_copies = []
    for k in range(chunks):
        src = tok_ref.at[pl.ds(k * piece, piece), :]
        for o in range(1, n_col):
            push(src, x_at(k, me), line_send.at[k, o], x_recv.at[k, me], dev_c[o])
        for o in range(1, n_depth):
            push(src, x_at(k, me), sib_send.at[k, o, 0], x_recv.at[k, me], dev_d[o])
        own = pltpu.make_async_copy(src, x_at(k, me), own_sem.at[k])
        own.start()
        own_copies.append(own)

    def gather_tokens(k):
        for o in range(1, n_col):
            block = cols[o] * n_depth + depth
            arrived(x_at(k, block), x_recv.at[k, block])
            for q in range(1, n_depth):
                push(x_at(k, block), x_at(k, block), sib_send.at[k, q, o], x_recv.at[k, block], dev_d[q])
        for q in range(1, n_depth):
            for o in range(n_col):
                block = cols[o] * n_depth + depths[q]
                arrived(x_at(k, block), x_recv.at[k, block])
        own_copies[k].wait()

    def up(k, j):
        value = jnp.dot(
            x_ref[pl.ds(k * chunk_rows, chunk_rows), :], w_ref[:, pl.ds(j * f_tile, f_tile)],
            preferred_element_type=f32,
        )
        part_ref[pl.ds(k * chunk_rows, chunk_rows), pl.ds(j * f_tile, f_tile)] = value.astype(bf16)
        push(rows_at(part_ref, k, row_z, j, 0), half_at(relay_a, k, j), rs_send.at[k, j, 0], rs_recv.at[k, j, 0], dev_x)
        push(rows_at(part_ref, k, row_z, j, 1), half_at(relay_b, k, j), rs_send.at[k, j, 1], rs_recv.at[k, j, 1], dev_y)
        push(rows_at(part_ref, k, row_x, j, 0), sum_at(from_x, k, j, 0), rs_send.at[k, j, 2], rs_recv.at[k, j, 2], dev_x)
        push(rows_at(part_ref, k, row_y, j, 1), sum_at(from_y, k, j, 1), rs_send.at[k, j, 3], rs_recv.at[k, j, 3], dev_y)

    def relay(k, j):
        arrived(half_at(relay_a, k, j), rs_recv.at[k, j, 0])
        mine = rows_at(part_ref, k, row_y, j, 0)[...].astype(f32)
        half_at(sum_a, k, j)[...] = (mine + half_at(relay_a, k, j)[...].astype(f32)).astype(bf16)
        push(half_at(sum_a, k, j), sum_at(from_y, k, j, 0), rs_send.at[k, j, 4], rs_recv.at[k, j, 4], dev_y)
        arrived(half_at(relay_b, k, j), rs_recv.at[k, j, 1])
        mine = rows_at(part_ref, k, row_x, j, 1)[...].astype(f32)
        half_at(sum_b, k, j)[...] = (mine + half_at(relay_b, k, j)[...].astype(f32)).astype(bf16)
        push(half_at(sum_b, k, j), sum_at(from_x, k, j, 1), rs_send.at[k, j, 5], rs_recv.at[k, j, 5], dev_x)

    def activate(k, j):
        arrived(sum_at(from_x, k, j, 0), rs_recv.at[k, j, 2])
        arrived(sum_at(from_y, k, j, 1), rs_recv.at[k, j, 3])
        arrived(sum_at(from_y, k, j, 0), rs_recv.at[k, j, 4])
        arrived(sum_at(from_x, k, j, 1), rs_recv.at[k, j, 5])
        span = pl.ds(j * f_tile, f_tile)
        mine = rows_at(part_ref, k, row, j)[...].astype(f32)
        rows = pl.ds(k * row_rows, row_rows)
        preact = mine + from_x[rows, span].astype(f32) + from_y[rows, span].astype(f32)
        value, slope = gelu_parts(preact)
        value = value.astype(bf16)
        grads = []
        for b in range(per_row):
            local = pl.ds(b * own_tokens + k * piece, piece)
            hid_ref[local, span] = value[b * piece:(b + 1) * piece]
            grads.append((cot_ref[local, span].astype(f32) * slope[b * piece:(b + 1) * piece]).astype(bf16))
        rows_at(g_ref, k, row, j)[...] = jnp.concatenate(grads, axis=0)
        spot = rows_at(g_ref, k, row, j)
        push(spot, spot, ag_send.at[k, j, 0], ag_recv.at[k, j, 0], dev_x)
        push(spot, spot, ag_send.at[k, j, 1], ag_recv.at[k, j, 1], dev_y)

    def forward(k, j):
        arrived(rows_at(g_ref, k, row_x, j), ag_recv.at[k, j, 0])
        spot = rows_at(g_ref, k, row_x, j, 0)
        push(spot, spot, ag_send.at[k, j, 2], ag_recv.at[k, j, 2], dev_y)
        arrived(rows_at(g_ref, k, row_y, j), ag_recv.at[k, j, 1])
        spot = rows_at(g_ref, k, row_y, j, 1)
        push(spot, spot, ag_send.at[k, j, 3], ag_recv.at[k, j, 3], dev_x)

    def gathered(k, j):
        arrived(rows_at(g_ref, k, row_z, j, 0), ag_recv.at[k, j, 2])
        arrived(rows_at(g_ref, k, row_z, j, 1), ag_recv.at[k, j, 3])

    def down(k, i):
        span = pl.ds(i * d_tile, d_tile)
        value = lax.dot_general(
            g_ref[pl.ds(k * chunk_rows, chunk_rows), :], w_ref[span, :],
            (((1,), (1,)), ((), ())), preferred_element_type=f32,
        ).astype(bf16)
        for c in range(n_col):
            for d in range(n_depth):
                start = (c * n_depth + d) * piece
                back_ref[k, d, pl.ds(c * piece, piece), span] = value[start:start + piece]
        for q in range(1, n_depth):
            push(
                back_ref.at[k, depths[q], :, span], sib_ref.at[q - 1, k, :, span],
                sb_send.at[k, i, q], sb_recv.at[k, i, q], dev_d[q],
            )

    def chip_sum(k, i):
        span = pl.ds(i * d_tile, d_tile)
        total = back_ref.at[k, depth][:, span].astype(f32)
        for q in range(1, n_depth):
            arrived(sib_ref.at[q - 1, k, :, span], sb_recv.at[k, i, q])
            total = total + sib_ref[q - 1, k, :, span].astype(f32)
        chip_ref[k, :, span] = total.astype(bf16)
        for o in range(1, n_col):
            push(
                chip_ref.at[k, pl.ds(al(cols[o] * piece, piece), piece), span],
                line_ref.at[o - 1, k, :, span],
                zl_send.at[k, i, o], zl_recv.at[k, i, o], dev_c[o],
            )

    def line_sum(k, i):
        span = pl.ds(i * d_tile, d_tile)
        total = chip_ref.at[k, pl.ds(al(col * piece, piece), piece), span][...].astype(f32)
        for o in range(1, n_col):
            arrived(line_ref.at[o - 1, k, :, span], zl_recv.at[k, i, o])
            total = total + line_ref[o - 1, k, :, span].astype(f32)
        ing_ref[pl.ds(k * piece, piece), span] = total.astype(bf16)

    gather_tokens(0)
    weight_copy.wait()
    for k in range(chunks):
        if k:
            gather_tokens(k)
        for j in range(nf):
            up(k, j)
            if j:
                relay(k, j - 1)
            if k:
                forward(k - 1, j)
        relay(k, nf - 1)
        if k:
            for j in range(nf):
                gathered(k - 1, j)
            for i in range(nd):
                down(k - 1, i)
                if i:
                    chip_sum(k - 1, i - 1)
            chip_sum(k - 1, nd - 1)
        for j in range(nf):
            activate(k, j)
    last = chunks - 1
    for j in range(nf):
        forward(last, j)
    for j in range(nf):
        gathered(last, j)
    for i in range(nd):
        down(last, i)
        if i:
            chip_sum(last, i - 1)
    chip_sum(last, nd - 1)
    for k in range(chunks):
        for i in range(nd):
            line_sum(k, i)
    for copy in sends:
        copy.wait_send()


def chain(n_row, n_col, n_depth, tokens, weight, cotangent):
    own_tokens, d_size = tokens.shape
    own_rows, f_size = cotangent.shape
    bf16 = jnp.bfloat16
    assert n_row == 4 and own_tokens % (16 * chunks) == 0
    blocks = n_col * n_depth
    all_tokens = own_tokens * blocks
    piece = own_tokens // chunks
    f_tile, d_tile = tile_of(f_size, 768), tile_of(d_size, 768)
    nf, nd = f_size // f_tile, d_size // d_tile
    whole = pl.BlockSpec(memory_space=pltpu.VMEM)
    dma = pltpu.SemaphoreType.DMA
    flops = 4 * all_tokens * d_size * f_size
    return pl.pallas_call(
        functools.partial(chain_kernel, n_row, n_col, n_depth, f_tile, d_tile),
        out_shape=[
            jax.ShapeDtypeStruct((own_rows, f_size), bf16),
            jax.ShapeDtypeStruct((own_tokens, d_size), bf16),
            jax.ShapeDtypeStruct((all_tokens, d_size), bf16),
            jax.ShapeDtypeStruct((all_tokens, f_size), bf16),
        ],
        in_specs=[whole, pl.BlockSpec(memory_space=pl.ANY), whole],
        out_specs=[whole] * 4,
        scratch_shapes=[
            pltpu.VMEM((d_size, f_size), bf16),
            pltpu.VMEM((all_tokens, f_size), bf16),
            pltpu.VMEM((own_rows // 2, f_size), bf16),
            pltpu.VMEM((own_rows // 2, f_size), bf16),
            pltpu.VMEM((own_rows // 2, f_size), bf16),
            pltpu.VMEM((own_rows // 2, f_size), bf16),
            pltpu.VMEM((own_rows, f_size), bf16),
            pltpu.VMEM((own_rows, f_size), bf16),
            pltpu.VMEM((chunks, n_depth, n_col * piece, d_size), bf16),
            pltpu.VMEM((n_depth - 1, chunks, n_col * piece, d_size), bf16),
            pltpu.VMEM((chunks, n_col * piece, d_size), bf16),
            pltpu.VMEM((n_col - 1, chunks, piece, d_size), bf16),
            dma, dma((chunks,)),
            dma((chunks, n_col)), dma((chunks, n_depth, n_col)), dma((chunks, blocks)),
            dma((chunks, nf, 6)), dma((chunks, nf, 6)),
            dma((chunks, nf, 4)), dma((chunks, nf, 4)),
            dma((chunks, nd, n_depth)), dma((chunks, nd, n_depth)),
            dma((chunks, nd, n_col)), dma((chunks, nd, n_col)),
        ],
        compiler_params=pltpu.CompilerParams(
            collective_id=0, has_side_effects=True, vmem_limit_bytes=62 * 2**20
        ),
        cost_estimate=pl.CostEstimate(
            flops=flops, bytes_accessed=2 * d_size * f_size, transcendentals=own_rows * f_size
        ),
        name="chain",
    )(tokens, weight, cotangent)


def weight_grad_kernel(scale, f_tile, x_ref, g_ref, out_ref):
    for j in range(g_ref.shape[1] // f_tile):
        span = pl.ds(j * f_tile, f_tile)
        out_ref[:, span] = scale * lax.dot_general(
            x_ref[...], g_ref[:, span], (((0,), (0,)), ((), ())),
            preferred_element_type=jnp.float32,
        )


def weight_grad_of(tokens, grads):
    count, d_size = tokens.shape
    f_size = grads.shape[1]
    d_tile, f_tile = tile_of(d_size, 256), tile_of(f_size, 768)
    return pl.pallas_call(
        functools.partial(weight_grad_kernel, count ** (-0.5), f_tile),
        grid=(d_size // d_tile,),
        out_shape=jax.ShapeDtypeStruct((d_size, f_size), jnp.float32),
        in_specs=[
            pl.BlockSpec((count, d_tile), lambda i: (0, i)),
            pl.BlockSpec((count, f_size), lambda i: (0, 0)),
        ],
        out_specs=pl.BlockSpec((d_tile, f_size), lambda i: (i, 0)),
        compiler_params=pltpu.CompilerParams(vmem_limit_bytes=40 * 2**20),
        cost_estimate=pl.CostEstimate(
            flops=2 * count * d_size * f_size, bytes_accessed=4 * d_size * f_size, transcendentals=0
        ),
        name="weight_grad",
    )(tokens, grads)


def solution(mesh):
    sizes = [mesh.shape[name] for name in ("row", "col", "depth")]

    def shards(tokens, weight, cotangent):
        hidden, input_grad, x_all, g_all = chain(*sizes, tokens, weight, cotangent)
        return (hidden, input_grad, weight_grad_of(x_all, g_all))

    in_specs = (P(("col", "depth"), "row"), P("row", ("col", "depth")), P("row", ("col", "depth")))
    out_specs = (P("row", ("col", "depth")), P(("col", "depth"), "row"), P("row", ("col", "depth")))
    return jax.shard_map(shards, mesh=mesh, in_specs=in_specs, out_specs=out_specs, check_vma=False)
```

```python
import functools

import jax
import jax.numpy as jnp
from jax import lax
from jax.experimental import pallas as pl
from jax.experimental.pallas import tpu as pltpu
from jax.sharding import PartitionSpec as P

MESH = pl.DeviceIdType.MESH
root_coef = 0.7978845608
cubic_coef = 0.044715
chunks = 2


def gelu_parts(preact):
    inner = root_coef * (preact + cubic_coef * preact * preact * preact)
    tanh_val = jnp.tanh(inner)
    value = 0.5 * preact * (1.0 + tanh_val)
    slope = 0.5 * (1.0 + tanh_val) + 0.5 * preact * (1.0 - tanh_val * tanh_val) * root_coef * (
        1.0 + 3.0 * cubic_coef * preact * preact
    )
    return (value, slope)


def tile_of(extent, most):
    return max(t for t in range(128, min(most, extent) + 1, 128) if extent % t == 0)


def chain_kernel(
    n_row, n_col, n_depth, f_tile, d_tile,
    tok_ref, w_hbm, cot_ref,
    hid_ref, ing_ref, tail_ref, x_ref, g_ref,
    w_ref, part_ref, relay_a, relay_b, sum_a, sum_b, from_x, from_y,
    back_ref, sib_ref, chip_ref, line_ref,
    w_sem, own_sem,
    line_send, sib_send, x_recv,
    rs_send, rs_recv, ag_send, ag_recv,
    sb_send, sb_recv, zl_send, zl_recv,
):
    f32, bf16 = jnp.float32, jnp.bfloat16
    row, col, depth = lax.axis_index("row"), lax.axis_index("col"), lax.axis_index("depth")
    blocks = n_col * n_depth
    own_tokens, d_size = tok_ref.shape
    f_size = cot_ref.shape[1]
    piece = own_tokens // chunks
    chunk_rows = blocks * piece
    row_rows = chunk_rows // n_row
    half = row_rows // 2
    per_row = blocks // n_row
    nf, nd = f_size // f_tile, d_size // d_tile

    row_x = row + 1 - 2 * lax.rem(row, 2)
    row_y = lax.rem(row + 2, 4)
    row_z = lax.rem(row_x + 2, 4)
    dev_x = (row_x, col, depth)
    dev_y = (row_y, col, depth)
    cols = [lax.rem(col + o, n_col) for o in range(n_col)]
    depths = [lax.rem(depth + o, n_depth) for o in range(n_depth)]
    dev_c = [(row, c, depth) for c in cols]
    dev_d = [(row, col, d) for d in depths]

    sends = []

    def push(src, dst, send_sem, recv_sem, device, when=None):
        copy = pltpu.make_async_remote_copy(
            src_ref=src, dst_ref=dst, send_sem=send_sem, recv_sem=recv_sem,
            device_id=device, device_id_type=MESH,
        )
        if when is None:
            copy.start()
        else:
            pl.when(when)(copy.start)
        sends.append((copy, when))

    def arrived(dst, recv_sem):
        pltpu.make_async_remote_copy(
            src_ref=dst, dst_ref=dst, send_sem=recv_sem, recv_sem=recv_sem,
            device_id=dev_x, device_id_type=MESH,
        ).wait_recv()

    def al(v, m):
        return pl.multiple_of(v, m)

    def x_at(k, block):
        return x_ref.at[pl.ds(al(k * chunk_rows + block * piece, piece), piece), :]

    def rows_at(ref, k, r, j, part=None):
        start = k * chunk_rows + r * row_rows
        size = row_rows
        if part is not None:
            start, size = start + part * half, half
        return ref.at[pl.ds(al(start, half), size), pl.ds(j * f_tile, f_tile)]

    def half_at(ref, k, j):
        return ref.at[pl.ds(k * half, half), pl.ds(j * f_tile, f_tile)]

    def sum_at(ref, k, j, part):
        return ref.at[pl.ds(k * row_rows + part * half, half), pl.ds(j * f_tile, f_tile)]

    weight_copy = pltpu.make_async_copy(w_hbm, w_ref, w_sem)
    weight_copy.start()

    barrier = pltpu.get_barrier_semaphore()
    greet = dev_c[1:] + dev_d[1:] + [dev_x, dev_y]
    for device in greet:
        pl.semaphore_signal(barrier, inc=1, device_id=device, device_id_type=MESH)
    pl.semaphore_wait(barrier, len(greet))

    me = col * n_depth + depth
    own_copies = []

    def start_tokens(k):
        src = tok_ref.at[pl.ds(k * piece, piece), :]

        push(src, x_at(k, me), line_send.at[k, 0, 0], x_recv.at[k, me], (row, col + 1, depth), col + 1 < n_col)
        push(src, x_at(k, me), line_send.at[k, 1, 0], x_recv.at[k, me], (row, col - 1, depth), col > 0)
        for q in range(1, n_depth):
            push(src, x_at(k, me), sib_send.at[k, q, 0, 0], x_recv.at[k, me], dev_d[q])
        own = pltpu.make_async_copy(src, x_at(k, me), own_sem.at[k])
        own.start()
        own_copies.append(own)

    def pass_tokens(k, s):
        for way, step in ((0, 1), (1, -1)):
            origin = col - step * (s + 1)
            here = jnp.logical_and(origin >= 0, origin < n_col)
            onward = jnp.logical_and(here, col + 1 < n_col if step == 1 else col > 0)

            block = jnp.clip(origin, 0, n_col - 1) * n_depth + depth
            spot, sem = x_at(k, block), x_recv.at[k, block]

            @pl.when(here)
            def _():
                arrived(spot, sem)

            if s < n_col - 2:
                push(spot, spot, line_send.at[k, way, s + 1], sem, (row, col + step, depth), onward)
            for q in range(1, n_depth):
                push(spot, spot, sib_send.at[k, q, way, s + 1], sem, dev_d[q], here)

    def finish_tokens(k):
        for q in range(1, n_depth):
            for o in range(n_col):
                block = cols[o] * n_depth + depths[q]
                arrived(x_at(k, block), x_recv.at[k, block])
        own_copies[k].wait()

    def up(k, j):
        value = jnp.dot(
            x_ref[pl.ds(k * chunk_rows, chunk_rows), :], w_ref[:, pl.ds(j * f_tile, f_tile)],
            preferred_element_type=f32,
        )
        part_ref[pl.ds(k * chunk_rows, chunk_rows), pl.ds(j * f_tile, f_tile)] = value.astype(bf16)
        push(rows_at(part_ref, k, row_z, j, 0), half_at(relay_a, k, j), rs_send.at[k, j, 0], rs_recv.at[k, j, 0], dev_x)
        push(rows_at(part_ref, k, row_z, j, 1), half_at(relay_b, k, j), rs_send.at[k, j, 1], rs_recv.at[k, j, 1], dev_y)
        push(rows_at(part_ref, k, row_x, j, 0), sum_at(from_x, k, j, 0), rs_send.at[k, j, 2], rs_recv.at[k, j, 2], dev_x)
        push(rows_at(part_ref, k, row_y, j, 1), sum_at(from_y, k, j, 1), rs_send.at[k, j, 3], rs_recv.at[k, j, 3], dev_y)

    def relay(k, j):
        arrived(half_at(relay_a, k, j), rs_recv.at[k, j, 0])
        mine = rows_at(part_ref, k, row_y, j, 0)[...].astype(f32)
        half_at(sum_a, k, j)[...] = (mine + half_at(relay_a, k, j)[...].astype(f32)).astype(bf16)
        push(half_at(sum_a, k, j), sum_at(from_y, k, j, 0), rs_send.at[k, j, 4], rs_recv.at[k, j, 4], dev_y)
        arrived(half_at(relay_b, k, j), rs_recv.at[k, j, 1])
        mine = rows_at(part_ref, k, row_x, j, 1)[...].astype(f32)
        half_at(sum_b, k, j)[...] = (mine + half_at(relay_b, k, j)[...].astype(f32)).astype(bf16)
        push(half_at(sum_b, k, j), sum_at(from_x, k, j, 1), rs_send.at[k, j, 5], rs_recv.at[k, j, 5], dev_x)

    def activate(k, j):
        arrived(sum_at(from_x, k, j, 0), rs_recv.at[k, j, 2])
        arrived(sum_at(from_y, k, j, 1), rs_recv.at[k, j, 3])
        arrived(sum_at(from_y, k, j, 0), rs_recv.at[k, j, 4])
        arrived(sum_at(from_x, k, j, 1), rs_recv.at[k, j, 5])
        span = pl.ds(j * f_tile, f_tile)
        mine = rows_at(part_ref, k, row, j)[...].astype(f32)
        rows = pl.ds(k * row_rows, row_rows)
        preact = mine + from_x[rows, span].astype(f32) + from_y[rows, span].astype(f32)
        value, slope = gelu_parts(preact)
        value = value.astype(bf16)
        grads = []
        for b in range(per_row):
            local = pl.ds(b * own_tokens + k * piece, piece)
            hid_ref[local, span] = value[b * piece:(b + 1) * piece]
            grads.append((cot_ref[local, span].astype(f32) * slope[b * piece:(b + 1) * piece]).astype(bf16))
        rows_at(g_ref, k, row, j)[...] = jnp.concatenate(grads, axis=0)
        spot = rows_at(g_ref, k, row, j)
        push(spot, spot, ag_send.at[k, j, 0], ag_recv.at[k, j, 0], dev_x)
        push(spot, spot, ag_send.at[k, j, 1], ag_recv.at[k, j, 1], dev_y)

    def forward(k, j):
        arrived(rows_at(g_ref, k, row_x, j), ag_recv.at[k, j, 0])
        spot = rows_at(g_ref, k, row_x, j, 0)
        push(spot, spot, ag_send.at[k, j, 2], ag_recv.at[k, j, 2], dev_y)
        arrived(rows_at(g_ref, k, row_y, j), ag_recv.at[k, j, 1])
        spot = rows_at(g_ref, k, row_y, j, 1)
        push(spot, spot, ag_send.at[k, j, 3], ag_recv.at[k, j, 3], dev_x)

    def gathered(k, j):
        arrived(rows_at(g_ref, k, row_z, j, 0), ag_recv.at[k, j, 2])
        arrived(rows_at(g_ref, k, row_z, j, 1), ag_recv.at[k, j, 3])

    def down(k, i):
        span = pl.ds(i * d_tile, d_tile)
        value = lax.dot_general(
            g_ref[pl.ds(k * chunk_rows, chunk_rows), :], w_ref[span, :],
            (((1,), (1,)), ((), ())), preferred_element_type=f32,
        ).astype(bf16)
        for c in range(n_col):
            for d in range(n_depth):
                start = (c * n_depth + d) * piece
                back_ref[k, d, pl.ds(c * piece, piece), span] = value[start:start + piece]
        for q in range(1, n_depth):
            push(
                back_ref.at[k, depths[q], :, span], sib_ref.at[q - 1, k, :, span],
                sb_send.at[k, i, q], sb_recv.at[k, i, q], dev_d[q],
            )

    def chip_sum(k, i):
        span = pl.ds(i * d_tile, d_tile)
        total = back_ref.at[k, depth][:, span].astype(f32)
        for q in range(1, n_depth):
            arrived(sib_ref.at[q - 1, k, :, span], sb_recv.at[k, i, q])
            total = total + sib_ref[q - 1, k, :, span].astype(f32)
        if k == chunks - 1:
            tail_ref[:, span] = total.astype(bf16)
            return
        chip_ref[k, :, span] = total.astype(bf16)
        for o in range(1, n_col):
            push(
                chip_ref.at[k, pl.ds(al(cols[o] * piece, piece), piece), span],
                line_ref.at[o - 1, k, :, span],
                zl_send.at[k, i, o], zl_recv.at[k, i, o], dev_c[o],
            )

    def line_sum(k, i):
        span = pl.ds(i * d_tile, d_tile)
        total = chip_ref.at[k, pl.ds(al(col * piece, piece), piece), span][...].astype(f32)
        for o in range(1, n_col):
            arrived(line_ref.at[o - 1, k, :, span], zl_recv.at[k, i, o])
            total = total + line_ref[o - 1, k, :, span].astype(f32)
        ing_ref[pl.ds(k * piece, piece), span] = total.astype(bf16)

    last = chunks - 1
    start_tokens(0)
    for s in range(n_col - 1):
        pass_tokens(0, s)
    for k in range(1, chunks):
        start_tokens(k)
    finish_tokens(0)
    weight_copy.wait()
    for k in range(chunks):
        passes = list(range(n_col - 1)) if k < last else []
        for j in range(nf):
            up(k, j)
            if j:
                relay(k, j - 1)
            if k:
                forward(k - 1, j)
            if passes and j == nf // 2:
                pass_tokens(k + 1, passes.pop(0))
        relay(k, nf - 1)
        if k:
            for j in range(nf):
                gathered(k - 1, j)
            for i in range(nd):
                down(k - 1, i)
                if i:
                    chip_sum(k - 1, i - 1)
            chip_sum(k - 1, nd - 1)
        for j in range(nf):
            activate(k, j)
            if passes:
                pass_tokens(k + 1, passes.pop(0))
        while passes:
            pass_tokens(k + 1, passes.pop(0))
        if k < last:
            finish_tokens(k + 1)
    for j in range(nf):
        forward(last, j)
    for k in range(last):
        for i in range(nd):
            line_sum(k, i)
    for j in range(nf):
        gathered(last, j)
    for i in range(nd):
        down(last, i)
        if i:
            chip_sum(last, i - 1)
    chip_sum(last, nd - 1)
    for copy, when in sends:
        if when is None:
            copy.wait_send()
        else:
            pl.when(when)(copy.wait_send)


def chain(n_row, n_col, n_depth, tokens, weight, cotangent):
    own_tokens, d_size = tokens.shape
    own_rows, f_size = cotangent.shape
    bf16 = jnp.bfloat16
    assert n_row == 4 and own_tokens % (16 * chunks) == 0
    blocks = n_col * n_depth
    all_tokens = own_tokens * blocks
    piece = own_tokens // chunks
    f_tile, d_tile = tile_of(f_size, 768), tile_of(d_size, 768)
    nf, nd = f_size // f_tile, d_size // d_tile
    whole = pl.BlockSpec(memory_space=pltpu.VMEM)
    dma = pltpu.SemaphoreType.DMA
    flops = 4 * all_tokens * d_size * f_size
    return pl.pallas_call(
        functools.partial(chain_kernel, n_row, n_col, n_depth, f_tile, d_tile),
        out_shape=[
            jax.ShapeDtypeStruct((own_rows, f_size), bf16),
            jax.ShapeDtypeStruct((own_tokens - piece, d_size), bf16),
            jax.ShapeDtypeStruct((n_col * piece, d_size), bf16),
            jax.ShapeDtypeStruct((all_tokens, d_size), bf16),
            jax.ShapeDtypeStruct((all_tokens, f_size), bf16),
        ],
        in_specs=[whole, pl.BlockSpec(memory_space=pl.ANY), whole],
        out_specs=[whole] * 5,
        scratch_shapes=[
            pltpu.VMEM((d_size, f_size), bf16),
            pltpu.VMEM((all_tokens, f_size), bf16),
            pltpu.VMEM((own_rows // 2, f_size), bf16),
            pltpu.VMEM((own_rows // 2, f_size), bf16),
            pltpu.VMEM((own_rows // 2, f_size), bf16),
            pltpu.VMEM((own_rows // 2, f_size), bf16),
            pltpu.VMEM((own_rows, f_size), bf16),
            pltpu.VMEM((own_rows, f_size), bf16),
            pltpu.VMEM((chunks, n_depth, n_col * piece, d_size), bf16),
            pltpu.VMEM((n_depth - 1, chunks, n_col * piece, d_size), bf16),
            pltpu.VMEM((chunks - 1, n_col * piece, d_size), bf16),
            pltpu.VMEM((n_col - 1, chunks - 1, piece, d_size), bf16),
            dma, dma((chunks,)),
            dma((chunks, 2, n_col)), dma((chunks, n_depth, 2, n_col)), dma((chunks, blocks)),
            dma((chunks, nf, 6)), dma((chunks, nf, 6)),
            dma((chunks, nf, 4)), dma((chunks, nf, 4)),
            dma((chunks, nd, n_depth)), dma((chunks, nd, n_depth)),
            dma((chunks, nd, n_col)), dma((chunks, nd, n_col)),
        ],
        compiler_params=pltpu.CompilerParams(
            collective_id=0, has_side_effects=True, vmem_limit_bytes=62 * 2**20
        ),
        cost_estimate=pl.CostEstimate(
            flops=flops, bytes_accessed=2 * d_size * f_size, transcendentals=own_rows * f_size
        ),
        name="chain",
    )(tokens, weight, cotangent)


def weight_grad_kernel(scale, f_tile, slots, parts, x_ref, g_ref, out_hbm, held, sems):
    step, steps = pl.program_id(0), pl.num_programs(0)
    rows = held.shape[1]
    size = rows // parts
    slot = lax.rem(step, slots)

    def piece_of(index, part):
        at = lax.rem(index, slots)
        return pltpu.make_async_copy(
            held.at[at, pl.ds(part * size, size), :],
            out_hbm.at[pl.ds(pl.multiple_of(index * rows + part * size, size), size), :],
            sems.at[at, part],
        )

    @pl.when(step >= slots)
    def _():
        for part in range(parts):
            piece_of(step - slots, part).wait()

    flipped = x_ref[...].T
    for part in range(parts):
        left = flipped[part * size:(part + 1) * size]
        for j in range(g_ref.shape[1] // f_tile):
            span = pl.ds(j * f_tile, f_tile)
            held[slot, pl.ds(part * size, size), span] = scale * jnp.dot(
                left, g_ref[:, span], preferred_element_type=jnp.float32
            )
        piece_of(step, part).start()

    @pl.when(step == steps - 1)
    def _():
        for back in range(slots):
            for part in range(parts):
                piece_of(step - back, part).wait()


def weight_grad_of(tokens, grads):
    count, d_size = tokens.shape
    f_size = grads.shape[1]
    d_tile, f_tile = tile_of(d_size, 512), tile_of(f_size, 768)
    slots, parts = 3, d_tile // tile_of(d_tile, 256)
    assert d_size // d_tile >= slots
    return pl.pallas_call(
        functools.partial(weight_grad_kernel, count ** (-0.5), f_tile, slots, parts),
        grid=(d_size // d_tile,),
        out_shape=jax.ShapeDtypeStruct((d_size, f_size), jnp.float32),
        in_specs=[
            pl.BlockSpec((count, d_tile), lambda i: (0, i)),
            pl.BlockSpec((count, f_size), lambda i: (0, 0)),
        ],
        out_specs=pl.BlockSpec(memory_space=pl.ANY),
        scratch_shapes=[
            pltpu.VMEM((slots, d_tile, f_size), jnp.float32),
            pltpu.SemaphoreType.DMA((slots, parts)),
        ],
        compiler_params=pltpu.CompilerParams(vmem_limit_bytes=60 * 2**20),
        cost_estimate=pl.CostEstimate(
            flops=2 * count * d_size * f_size, bytes_accessed=4 * d_size * f_size, transcendentals=0
        ),
        name="weight_grad",
    )(tokens, grads)


def solution(mesh):
    sizes = [mesh.shape[name] for name in ("row", "col", "depth")]

    def shards(tokens, weight, cotangent):
        hidden, early, tail, x_all, g_all = chain(*sizes, tokens, weight, cotangent)
        late = lax.psum_scatter(tail, "col", scatter_dimension=0, tiled=True)
        weight_grad = weight_grad_of(x_all, g_all)
        return (hidden, jnp.concatenate([early, late], axis=0), weight_grad)

    in_specs = (P(("col", "depth"), "row"), P("row", ("col", "depth")), P("row", ("col", "depth")))
    out_specs = (P("row", ("col", "depth")), P(("col", "depth"), "row"), P("row", ("col", "depth")))
    return jax.shard_map(shards, mesh=mesh, in_specs=in_specs, out_specs=out_specs, check_vma=False)
```
